32 devices in a mesh: neuron: 8 (over z, y), tm: 4 (over x, core).
Axes of the slice: x: 2, y: 2, z: 4, core: 2. Of those that a mesh axis runs over, the one named last changes fastest.
Arguments:
- data: bfloat16 [1024, 8192], P('neuron', 'tm'), may hold values from 0 to 2
- behaviour: bfloat16 [512, 8192], P('neuron', 'tm'), may hold values from 0 to 2
- motifs: bfloat16 [32, 1024, 128], P('tm', 'neuron'), may hold values from 0 to 2
- behav_motifs: bfloat16 [32, 512, 128], P('tm', 'neuron'), may hold values from 0 to 2
- activations: bfloat16 [128, 8192], P(None, 'tm'), may hold values from 0 to 2
Outputs:
- new_motifs: bfloat16 [32, 1024, 128], P('tm', 'neuron')
- new_behav_motifs: bfloat16 [32, 512, 128], P('tm', 'neuron')
- new_activations: bfloat16 [128, 8192], P(None, 'tm')
The draws below stay inside these ranges and needn't reach their ends.
All inputs are finite; a program needn't handle non-finite values.
Results may differ from the reference program's by a relative error of at most 0.0034.
Values may be sent and summed in bfloat16 or wider, within the bound.
A program may use at most 64 MiB of HBM per device.

```python
import math
import jax
import jax.numpy as jnp
from jax import lax

K = 128
L = 32
F = 512
NN = 1024
NT = 8192


def levels(own_key, extent, pieces, least, largest):
    gain, own = 1.0, jax.random.fold_in(own_key, 6)
    for axis_at, blocks in pieces:
        heights = jnp.exp(jax.random.uniform(jax.random.fold_in(own, axis_at), (blocks,), jnp.float32, least / len(pieces), largest / len(pieces)))
        gain = gain * jnp.repeat(heights, extent[axis_at] // blocks).reshape([-1 if axis == axis_at else 1 for axis in range(len(extent))])
    return gain


def setup_inputs(seed: int = 0) -> dict:
    keys = jax.random.split(jax.random.key(seed), 6)
    return {
        "data": jnp.clip(2.0 * jax.random.uniform(keys[0], (NN, NT), jnp.float32) ** levels(keys[0], (NN, NT), ((0, 8), (1, 4)), -0.2, 0.2), 0.0, 2.0).astype(jnp.bfloat16),
        "behaviour": jnp.clip(2.0 * jax.random.uniform(keys[1], (F, NT), jnp.float32) ** levels(keys[1], (F, NT), ((0, 8), (1, 4)), -0.2, 0.2), 0.0, 2.0).astype(jnp.bfloat16),
        "motifs": jnp.clip(2.0 * jax.random.uniform(keys[2], (L, NN, K), jnp.float32) ** levels(keys[2], (L, NN, K), ((0, 4), (1, 8)), -0.2, 0.2), 0.0, 2.0).astype(jnp.bfloat16),
        "behav_motifs": jnp.clip(2.0 * jax.random.uniform(keys[3], (L, F, K), jnp.float32) ** levels(keys[3], (L, F, K), ((0, 4), (1, 8)), -0.2, 0.2), 0.0, 2.0).astype(jnp.bfloat16),
        "activations": jnp.clip(2.0 * jax.random.uniform(keys[4], (K, NT), jnp.float32) ** levels(keys[4], (K, NT), ((1, 4),), -0.2, 0.2), 0.0, 2.0).astype(jnp.bfloat16),
    }


def reference(data, behaviour, motifs, behav_motifs, activations):
    scale = 1.0 / (L * K)
    rate_motif = 0.5 * L * K / math.sqrt(NT)
    rate_active = 0.5 * L * K / math.sqrt(L * (NN + 4 * F))
    rim = L - 1
    extended = jnp.concatenate([jnp.zeros((K, rim), activations.dtype), activations], axis=1)
    lag_list = jnp.arange(L, dtype=jnp.int32)

    def window(lag):
        return lax.dynamic_slice_in_dim(extended, rim - lag, NT, 1)

    def forward(acc, lag):
        win = window(lag)
        neuron_rows = lax.dynamic_index_in_dim(motifs, lag, 0, keepdims=False)
        feature_rows = lax.dynamic_index_in_dim(behav_motifs, lag, 0, keepdims=False)
        return ((acc[0] + jnp.dot(neuron_rows, win, preferred_element_type=jnp.float32), acc[1] + jnp.dot(feature_rows, win, preferred_element_type=jnp.float32)), None)
    start_pair = (jnp.zeros((NN, NT), jnp.float32), jnp.zeros((F, NT), jnp.float32))
    (recon_x, recon_b), _ = lax.scan(forward, start_pair, lag_list)
    resid_x = (data.astype(jnp.float32) - scale * recon_x).astype(jnp.bfloat16)
    resid_b = (2.0 * (behaviour.astype(jnp.float32) - scale * recon_b)).astype(jnp.bfloat16)

    def motif_grad(lag):
        win = window(lag)
        neuron_part = lax.dot_general(resid_x, win, (((1,), (1,)), ((), ())), preferred_element_type=jnp.float32)
        feature_part = lax.dot_general(resid_b, win, (((1,), (1,)), ((), ())), preferred_element_type=jnp.float32)
        return (-scale * neuron_part, -scale * feature_part)
    grad_w, grad_v = lax.map(motif_grad, lag_list)

    def backward(acc, lag):
        neuron_rows = lax.dynamic_index_in_dim(motifs, lag, 0, keepdims=False)
        feature_rows = lax.dynamic_index_in_dim(behav_motifs, lag, 0, keepdims=False)
        back = lax.dot_general(neuron_rows, resid_x, (((0,), (0,)), ((), ())), preferred_element_type=jnp.float32)
        back = back + lax.dot_general(feature_rows, resid_b, (((0,), (0,)), ((), ())), preferred_element_type=jnp.float32)
        place = rim - lag
        current = lax.dynamic_slice_in_dim(acc, place, NT, 1)
        return (lax.dynamic_update_slice_in_dim(acc, current + back, place, 1), None)
    extended_back, _ = lax.scan(backward, jnp.zeros((K, rim + NT), jnp.float32), lag_list)
    grad_h = -scale * extended_back[:, rim:]
    new_motifs = jnp.maximum(motifs.astype(jnp.float32) - rate_motif * grad_w, 0.0).astype(jnp.bfloat16)
    new_behav = jnp.maximum(behav_motifs.astype(jnp.float32) - rate_motif * grad_v, 0.0).astype(jnp.bfloat16)
    new_active = jnp.maximum(activations.astype(jnp.float32) - rate_active * grad_h, 0.0).astype(jnp.bfloat16)
    return (new_motifs, new_behav, new_active)
```

```python
import functools
import math

import jax
import jax.numpy as jnp
from jax import lax
from jax.experimental import pallas as pl
from jax.experimental.pallas import tpu as pltpu
from jax.sharding import PartitionSpec as P

behaviour_weight = 2.0
LANES = 128
MESH = pl.DeviceIdType.MESH
F32 = jnp.float32
BF16 = jnp.bfloat16


def remote(src, dst, send, recv, **where):
    return pltpu.make_async_remote_copy(
        src_ref=src, dst_ref=dst, send_sem=send, recv_sem=recv,
        device_id=where, device_id_type=MESH,
    )


def kernel(
    peers, direct, scale, rate_motif, rate_active, neurons, features, rows,
    data, beh, mot, bmot, act, o_mot, o_bmot, o_act,
    h_ext, ext, wst, wf, wt, acc, rext, r8, gbuf, gin, gown, gx, gx_in,
    halo_sem, w_send, w_recv, g_send, g_recv, *rest,
):
    lags = mot.shape[0]
    width, frames = act.shape
    groups = 4
    wide = lags * width
    me = lax.axis_index("tm")
    chip, core = me // 2, me % 2
    partner = 2 * chip + (1 - core)
    across = 2 * (1 - chip) + core
    diag = 2 * (1 - chip) + (1 - core)
    row = lax.axis_index("neuron")
    if direct:
        (hs, ph, ha1, hb1, ha2, hb2, sa, sb, pa, pb, y_send, y_recv, b1_send, b1_recv, a2_send,
         a2_recv, oaz_send, oaz_recv, oay_send, oay_recv, obz_send, obz_recv) = rest

    for j in range(lags):
        wst[me, j, :neurons, :] = mot[j]
        tail = bmot[j]
        if rows - neurons > features:
            tail = jnp.concatenate(
                [tail, jnp.zeros((rows - neurons - features, width), BF16)], axis=0)
        wst[me, j, neurons:, :] = tail

    barrier = pltpu.get_barrier_semaphore()
    for other in (partner, across, diag):
        pl.semaphore_signal(barrier, inc=1, device_id={"tm": other}, device_id_type=MESH)

    greeted = 3
    if direct:
        outer = peers // 2
        near = [row // 2 * 2 + 1 - row % 2]
        near += [(row // 2 + d) % outer * 2 + row % 2 for d in range(1, outer)]
        for other in near:
            pl.semaphore_signal(
                barrier, inc=1, device_id={"neuron": other}, device_id_type=MESH)
        greeted += len(near)
    pl.semaphore_wait(barrier, greeted)

    act_halo = remote(act.at[:, frames - LANES:], ext.at[:, :LANES],
                      halo_sem.at[0], halo_sem.at[1], tm=(me + 1) % groups)
    pl.when(me < groups - 1)(act_halo.start)
    w_across = remote(wst.at[me], wst.at[me], w_send.at[0], w_recv.at[0], tm=across)
    w_across.start()
    w_partner = remote(wst.at[me], wst.at[me], w_send.at[1], w_recv.at[1], tm=partner)
    w_partner.start()
    w_relay = remote(wst.at[across], wst.at[across], w_send.at[2], w_recv.at[2], tm=partner)

    ext[:, LANES:] = act[...]

    @pl.when(me == 0)
    def _():
        ext[:, :LANES] = jnp.zeros((width, LANES), BF16)

    pl.when(me > 0)(act_halo.wait_recv)

    def spread(b, c):
        at = pl.multiple_of(b * 16, 16)
        x = ext[pl.ds(at, 16), :]
        for lag in range(groups * lags):
            y = x if lag == 0 else pltpu.roll(x, lag, 1)
            h_ext[pl.ds(lag * width + at, 16), :] = y[:, LANES:]
        return c

    lax.fori_loop(0, width // 16, spread, 0)

    step = 512

    def side(g):
        for j in range(lags):
            wf[:, j * width:(j + 1) * width] = wst[g, j]
        wt[pl.ds(pl.multiple_of(g * width, width), width), :] = (
            wst[g].reshape(lags * rows, width).T)

    def forward(g, first, last):
        side(g)
        base = pl.multiple_of(g * wide, wide)

        def body(c, carry):
            cols = pl.ds(pl.multiple_of(c * step, step), step)
            v = jnp.dot(wf[...], h_ext[pl.ds(base, wide), cols], preferred_element_type=F32)
            if not first:
                v = acc[:, cols] + v
            if not last:
                acc[:, cols] = v
                return carry
            rext[:neurons, cols] = (
                data[:, cols].astype(F32) - scale * v[:neurons]).astype(BF16)
            tail = (behaviour_weight * (
                beh[:, cols].astype(F32) - scale * v[neurons:neurons + features])).astype(BF16)
            if rows - neurons > features:
                tail = jnp.concatenate(
                    [tail, jnp.zeros((rows - neurons - features, step), BF16)], axis=0)
            rext[neurons:, cols] = tail
            return carry

        if not last:
            lax.fori_loop(0, frames // step, body, 0)
            return
        body(0, 0)
        pl.when(me > 0)(r_halo.start)
        lax.fori_loop(1, frames // step, body, 0)

    r_halo = remote(rext.at[:, :LANES], rext.at[:, frames:],
                    halo_sem.at[2], halo_sem.at[3], tm=(me + groups - 1) % groups)
    forward(me, True, False)
    w_partner.wait_recv()
    forward(partner, False, False)
    w_across.wait_recv()
    w_relay.start()
    forward(across, False, False)
    w_relay.wait_recv()
    forward(diag, False, True)

    @pl.when(me == groups - 1)
    def _():
        rext[:, frames:] = jnp.zeros((rows, LANES), BF16)

    pl.when(me < groups - 1)(r_halo.wait_recv)

    def spread_back(b, c):
        at = pl.multiple_of(b * 16, 16)
        x = rext[pl.ds(at, 16), :]
        for j in range(lags):
            y = x if j == 0 else pltpu.roll(x, frames + LANES - j, 1)
            r8[pl.ds(j * rows + at, 16), :] = y
        return c

    lax.fori_loop(0, rows // 16, spread_back, 0)

    def back(c):
        at = pl.multiple_of(c * step, step)
        v = jnp.dot(wt[...], r8[:, pl.ds(at, step + LANES)], preferred_element_type=F32)
        total = v[:width, :step]
        for g in range(1, groups):
            total = total + v[g * width:(g + 1) * width, g * lags:g * lags + step]
        if not direct:
            o_act[:, pl.ds(at, step)] = total
            return
        ph[:, pl.ds(at, step)] = total
        mean, rest = centred(total)
        hs[:width, pl.ds(at, step)] = rest
        hs[width:, pl.ds(at, step)] = mean

    def centred(total):
        mean = jnp.mean(total, axis=0, keepdims=True).astype(BF16)
        rest = (total - mean.astype(F32)).astype(BF16)
        return jnp.broadcast_to(mean, (16, total.shape[1])), rest

    def whole(part):
        return part[:width].astype(F32) + part[width:width + 1].astype(F32)

    def fresh(at, total):
        lanes = pl.ds(at, LANES)
        o_act[:, lanes] = jnp.maximum(
            act[:, lanes].astype(F32) + (rate_active * scale) * total, 0.0).astype(BF16)

    if not direct:
        for c in range(frames // step):
            back(c)
    else:
        half = frames // 2
        quarter = frames // 4
        outer = peers // 2
        inner, far = row % 2, row // 2
        beside = far * 2 + (1 - inner)
        others = [(far + d) % outer for d in range(1, outer)]
        pair = half // outer

        def lanes_at(at, size):
            return pl.ds(pl.multiple_of(at, LANES), size)

        def first_b(to, sender):
            return remote(hs.at[:, lanes_at(half + to * pair, pair)], hb1.at[sender],
                          b1_send.at[to], b1_recv.at[sender], neuron=to * 2 + inner)

        a1 = remote(hs.at[:, lanes_at((1 - inner) * quarter, quarter)], ha1,
                    y_send.at[0], y_recv.at[0], neuron=beside)

        back(2)
        back(3)
        for z in others:
            first_b(z, far).start()
        back(1 - inner)
        a1.start()
        back(inner)

        def second_a(to, sender):
            return remote(sa.at[:, lanes_at(to * LANES, LANES)], ha2.at[sender],
                          a2_send.at[to], a2_recv.at[sender], neuron=to * 2 + inner)

        b2 = remote(sb.at[:, lanes_at((1 - inner) * LANES, LANES)], hb2,
                    y_send.at[1], y_recv.at[1], neuron=beside)

        def stage_two():
            a1.wait_recv()
            total = ph[:, lanes_at(inner * quarter, quarter)] + whole(ha1[...])
            pa[...] = total
            sa[width:], sa[:width] = centred(total)
            for z in others:
                second_a(z, far).start()
            total = ph[:, lanes_at(half + far * pair, pair)]
            for z in others:
                first_b(far, z).wait_recv()
                total = total + whole(hb1[z])
            pb[...] = total
            sb[width:], sb[:width] = centred(total)
            b2.start()

        def place_a(z, y):
            return pl.multiple_of(y * quarter + z * LANES, LANES)

        def place_b(z, y):
            return pl.multiple_of(half + z * pair + y * LANES, LANES)

        def out_copy(at, send, recv, to):
            piece = o_act.at[:, pl.ds(at, LANES)]
            return remote(piece, piece, send, recv, neuron=to)

        def az(to, owner):
            return out_copy(place_a(owner, inner), oaz_send.at[to], oaz_recv.at[owner],
                            to * 2 + inner)

        def ay(z, y):
            return out_copy(place_a(z, y), oay_send.at[z], oay_recv.at[z], beside)

        def by(y):
            return out_copy(place_b(far, y), y_send.at[2], y_recv.at[2], beside)

        def bz(to, owner, y, slot):
            return out_copy(place_b(owner, y), obz_send.at[slot, to], obz_recv.at[slot, owner],
                            to * 2 + inner)

        def stage_three():
            total = pa[:, lanes_at(far * LANES, LANES)]
            for z in others:
                second_a(far, z).wait_recv()
                total = total + whole(ha2[z])
            fresh(place_a(far, inner), total)
            for z in others:
                az(z, far).start()
            ay(far, inner).start()
            b2.wait_recv()
            fresh(place_b(far, inner), pb[:, lanes_at(inner * LANES, LANES)] + whole(hb2[...]))
            by(inner).start()
            for z in others:
                bz(z, far, inner, 0).start()

        def stage_four():
            by(1 - inner).wait_recv()
            for z in others:
                bz(z, far, 1 - inner, 1).start()
            for z in others:
                az(far, z).wait_recv()
                ay(z, inner).start()

        def stage_five():
            for z in others:
                bz(far, z, inner, 0).wait_recv()
                bz(far, z, 1 - inner, 1).wait_recv()
            for z in range(outer):
                ay(z, 1 - inner).wait_recv()
                ay(z, inner).wait_send()
            for z in others:
                first_b(z, far).wait_send()
                second_a(z, far).wait_send()
                az(z, far).wait_send()
                bz(z, far, inner, 0).wait_send()
                bz(z, far, 1 - inner, 1).wait_send()
            a1.wait_send()
            b2.wait_send()
            by(inner).wait_send()

    def grad(g, buffer):
        base = pl.multiple_of(g * wide, wide)

        def body(c, carry):
            at = pl.multiple_of(c * 256, 256)
            buffer[:, pl.ds(at, 256)] = lax.dot_general(
                rext[:, :frames], h_ext[pl.ds(base + at, 256), :],
                (((1,), (1,)), ((), ())), preferred_element_type=F32)
            return carry

        lax.fori_loop(0, wide // 256, body, 0)

    grad(diag, gbuf.at[0])
    g_diag = remote(gbuf.at[0], gin.at[0], g_send.at[0], g_recv.at[0], tm=partner)
    g_diag.start()
    if direct:
        stage_two()
    grad(across, gown)
    g_diag.wait_recv()
    total = gown[...] + gin[0]
    mean = jnp.mean(total, axis=1, keepdims=True).astype(BF16)
    gx[:, :wide] = (total - mean.astype(F32)).astype(BF16)
    gx[:, wide:] = jnp.broadcast_to(mean, (rows, LANES))
    g_across = remote(gx, gx_in, g_send.at[1], g_recv.at[1], tm=across)
    g_across.start()
    if direct:
        stage_three()
    grad(partner, gbuf.at[1])
    g_partner = remote(gbuf.at[1], gin.at[1], g_send.at[2], g_recv.at[2], tm=partner)
    g_partner.start()
    if direct:
        stage_four()
    grad(me, gown)
    g_partner.wait_recv()
    g_across.wait_recv()
    back_mean = gx_in[:, wide:].astype(F32)
    for j in range(lags):
        cols = slice(j * width, (j + 1) * width)
        g = gown[:, cols] + gin[1, :, cols] + (gx_in[:, cols].astype(F32) + back_mean)
        g = (rate_motif * scale) * g
        o_mot[j] = jnp.maximum(mot[j].astype(F32) + g[:neurons], 0.0).astype(BF16)
        o_bmot[j] = jnp.maximum(
            bmot[j].astype(F32) + g[neurons:neurons + features], 0.0).astype(BF16)
    if direct:
        stage_five()
    pl.when(me < groups - 1)(act_halo.wait_send)
    pl.when(me > 0)(r_halo.wait_send)
    for copy in (w_across, w_partner, w_relay, g_diag, g_across, g_partner):
        copy.wait_send()


def local(peers, groups, data, behaviour, motifs, behav_motifs, activations):
    lags, neurons, width = motifs.shape
    features = behaviour.shape[0]
    frames = activations.shape[1]
    lag_count = lags * groups
    scale = 1.0 / (lag_count * width)
    rate_motif = 0.5 * lag_count * width / math.sqrt(frames * groups)
    rate_active = 0.5 * lag_count * width / math.sqrt(
        lag_count * (neurons * peers + 4 * features * peers))
    rows = neurons + -(-features // 16) * 16
    wide = lags * width
    direct = frames // (2 * peers) == LANES and peers % 2 == 0
    outer = max(peers // 2, 1)
    dma = pltpu.SemaphoreType.DMA
    vmem = pl.BlockSpec(memory_space=pltpu.VMEM)
    flops = 6 * rows * lag_count * width * frames
    scratch = [
        pltpu.VMEM((lag_count * width, frames), BF16),
        pltpu.VMEM((width, frames + LANES), BF16),
        pltpu.VMEM((groups, lags, rows, width), BF16),
        pltpu.VMEM((rows, wide), BF16),
        pltpu.VMEM((groups * width, lags * rows), BF16),
        pltpu.VMEM((rows, frames), F32),
        pltpu.VMEM((rows, frames + LANES), BF16),
        pltpu.VMEM((lags * rows, frames + LANES), BF16),
        pltpu.VMEM((2, rows, wide), F32),
        pltpu.VMEM((2, rows, wide), F32),
        pltpu.VMEM((rows, wide), F32),
        pltpu.VMEM((rows, wide + LANES), BF16),
        pltpu.VMEM((rows, wide + LANES), BF16),
        dma((4,)), dma((3,)), dma((3,)), dma((3,)), dma((3,)),
    ]
    if direct:
        tall, quarter, pair = width + 16, frames // 4, frames // 2 // outer
        scratch += [
            pltpu.VMEM((tall, frames), BF16),
            pltpu.VMEM((width, frames), F32),
            pltpu.VMEM((tall, quarter), BF16),
            pltpu.VMEM((outer, tall, pair), BF16),
            pltpu.VMEM((outer, tall, LANES), BF16),
            pltpu.VMEM((tall, LANES), BF16),
            pltpu.VMEM((tall, quarter), BF16),
            pltpu.VMEM((tall, pair), BF16),
            pltpu.VMEM((width, quarter), F32),
            pltpu.VMEM((width, pair), F32),
            dma((3,)), dma((3,)),
            dma((outer,)), dma((outer,)), dma((outer,)), dma((outer,)),
            dma((outer,)), dma((outer,)), dma((outer,)), dma((outer,)),
            dma((2, outer)), dma((2, outer)),
        ]
    out = pl.pallas_call(
        functools.partial(kernel, peers, direct, scale, rate_motif, rate_active,
                          neurons, features, rows),
        out_shape=(
            jax.ShapeDtypeStruct(motifs.shape, BF16),
            jax.ShapeDtypeStruct(behav_motifs.shape, BF16),
            jax.ShapeDtypeStruct(activations.shape, BF16 if direct else F32),
        ),
        in_specs=[vmem] * 5,
        out_specs=[vmem] * 3,
        scratch_shapes=scratch,
        compiler_params=pltpu.CompilerParams(
            collective_id=0, has_side_effects=True, vmem_limit_bytes=60 * 1024 * 1024),
        cost_estimate=pl.CostEstimate(
            flops=flops, bytes_accessed=4 * 1024 * 1024, transcendentals=0),
    )(data, behaviour, motifs, behav_motifs, activations)
    if direct:
        return out
    grad = (rate_active * scale) * lax.psum(out[2], "neuron")
    return out[0], out[1], jnp.maximum(activations.astype(F32) + grad, 0.0).astype(BF16)


def solution(mesh):
    placed = (
        P("neuron", "tm"),
        P("neuron", "tm"),
        P("tm", "neuron", None),
        P("tm", "neuron", None),
        P(None, "tm"),
    )
    return jax.shard_map(
        functools.partial(local, mesh.shape["neuron"], mesh.shape["tm"]),
        mesh=mesh,
        in_specs=placed,
        out_specs=(P("tm", "neuron", None), P("tm", "neuron", None), P(None, "tm")),
        check_vma=False,
    )
```

```python
import functools
import math

import jax
import jax.numpy as jnp
from jax import lax
from jax.experimental import pallas as pl
from jax.experimental.pallas import tpu as pltpu
from jax.sharding import PartitionSpec as P

behaviour_weight = 2.0
LANES = 128
MESH = pl.DeviceIdType.MESH
F32 = jnp.float32
BF16 = jnp.bfloat16


def remote(src, dst, send, recv, **where):
    return pltpu.make_async_remote_copy(
        src_ref=src, dst_ref=dst, send_sem=send, recv_sem=recv,
        device_id=where, device_id_type=MESH,
    )


def kernel(
    peers, direct, scale, rate_motif, rate_active, neurons, features, rows,
    data, beh, mot, bmot, act, o_mot, o_bmot, o_act,
    h_ext, ext, wst, wf, wt, acc, rext, r8, gbuf, gin, gown, gx, gx_in,
    halo_sem, w_send, w_recv, g_send, g_recv, *rest,
):
    lags = mot.shape[0]
    width, frames = act.shape
    groups = 4
    wide = lags * width
    me = lax.axis_index("tm")
    chip, core = me // 2, me % 2
    partner = 2 * chip + (1 - core)
    across = 2 * (1 - chip) + core
    diag = 2 * (1 - chip) + (1 - core)
    row = lax.axis_index("neuron")
    if direct:
        (hs, ph, ha1, hb1, ha2, hb2, sa, sb, pa, pb, y_send, y_recv, b1_send, b1_recv, a2_send,
         a2_recv, oaz_send, oaz_recv, oay_send, oay_recv, obz_send, obz_recv) = rest

    for j in range(lags):
        wst[me, j, :neurons, :] = mot[j]
        tail = bmot[j]
        if rows - neurons > features:
            tail = jnp.concatenate(
                [tail, jnp.zeros((rows - neurons - features, width), BF16)], axis=0)
        wst[me, j, neurons:, :] = tail

    barrier = pltpu.get_barrier_semaphore()
    for other in (partner, across, diag):
        pl.semaphore_signal(barrier, inc=1, device_id={"tm": other}, device_id_type=MESH)

    greeted = 3
    if direct:
        outer = peers // 2
        near = [row // 2 * 2 + 1 - row % 2]
        near += [(row // 2 + d) % outer * 2 + row % 2 for d in range(1, outer)]
        for other in near:
            pl.semaphore_signal(
                barrier, inc=1, device_id={"neuron": other}, device_id_type=MESH)
        greeted += len(near)
    pl.semaphore_wait(barrier, greeted)

    act_halo = remote(act.at[:, frames - LANES:], ext.at[:, :LANES],
                      halo_sem.at[0], halo_sem.at[1], tm=(me + 1) % groups)
    pl.when(me < groups - 1)(act_halo.start)
    w_across = remote(wst.at[me], wst.at[me], w_send.at[0], w_recv.at[0], tm=across)
    w_across.start()
    w_partner = remote(wst.at[me], wst.at[me], w_send.at[1], w_recv.at[1], tm=partner)
    w_partner.start()
    w_relay = remote(wst.at[across], wst.at[across], w_send.at[2], w_recv.at[2], tm=partner)

    ext[:, LANES:] = act[...]

    @pl.when(me == 0)
    def _():
        ext[:, :LANES] = jnp.zeros((width, LANES), BF16)

    pl.when(me > 0)(act_halo.wait_recv)

    def spread(b, c):
        at = pl.multiple_of(b * 16, 16)
        x = ext[pl.ds(at, 16), :]
        for lag in range(groups * lags):
            y = x if lag == 0 else pltpu.roll(x, lag, 1)
            h_ext[pl.ds(lag * width + at, 16), :] = y[:, LANES:]
        return c

    lax.fori_loop(0, width // 16, spread, 0)

    step = frames // 2

    def side(g):
        for j in range(lags):
            wf[:, j * width:(j + 1) * width] = wst[g, j]
        wt[pl.ds(pl.multiple_of(g * width, width), width), :] = (
            wst[g].reshape(lags * rows, width).T)

    def forward(g, first, last):
        side(g)
        base = pl.multiple_of(g * wide, wide)

        def body(at, size):
            cols = slice(at, at + size)
            v = jnp.dot(wf[...], h_ext[pl.ds(base, wide), cols], preferred_element_type=F32)
            if not first:
                v = acc[:, cols] + v
            if not last:
                acc[:, cols] = v
                return
            rext[:neurons, cols] = (
                data[:, cols].astype(F32) - scale * v[:neurons]).astype(BF16)
            tail = (behaviour_weight * (
                beh[:, cols].astype(F32) - scale * v[neurons:neurons + features])).astype(BF16)
            if rows - neurons > features:
                tail = jnp.concatenate(
                    [tail, jnp.zeros((rows - neurons - features, size), BF16)], axis=0)
            rext[neurons:, cols] = tail

        if not last:
            body(0, frames)
            return
        body(0, step)
        pl.when(me > 0)(r_halo.start)
        body(step, frames - step)

    r_halo = remote(rext.at[:, :LANES], rext.at[:, frames:],
                    halo_sem.at[2], halo_sem.at[3], tm=(me + groups - 1) % groups)
    forward(me, True, False)
    w_partner.wait_recv()
    forward(partner, False, False)
    w_across.wait_recv()
    w_relay.start()
    forward(across, False, False)
    w_relay.wait_recv()
    forward(diag, False, True)

    @pl.when(me == groups - 1)
    def _():
        rext[:, frames:] = jnp.zeros((rows, LANES), BF16)

    pl.when(me < groups - 1)(r_halo.wait_recv)

    def spread_back(b, c):
        at = pl.multiple_of(b * 16, 16)
        x = rext[pl.ds(at, 16), :]
        for j in range(lags):
            y = x if j == 0 else pltpu.roll(x, frames + LANES - j, 1)
            r8[pl.ds(j * rows + at, 16), :] = y
        return c

    lax.fori_loop(0, rows // 16, spread_back, 0)

    def back(c):
        at = c * step
        v = jnp.dot(wt[...], r8[:, pl.ds(at, step + LANES)], preferred_element_type=F32)
        total = v[:width, :step]
        for g in range(1, groups):
            total = total + v[g * width:(g + 1) * width, g * lags:g * lags + step]
        if not direct:
            o_act[:, pl.ds(at, step)] = total
            return
        ph[:, pl.ds(at, step)] = total
        mean, rest = centred(total)
        hs[:width, pl.ds(at, step)] = rest
        hs[width:, pl.ds(at, step)] = mean

    def centred(total):
        mean = jnp.mean(total, axis=0, keepdims=True).astype(BF16)
        rest = (total - mean.astype(F32)).astype(BF16)
        return jnp.broadcast_to(mean, (16, total.shape[1])), rest

    def whole(part):
        return part[:width].astype(F32) + part[width:width + 1].astype(F32)

    def fresh(at, total):
        lanes = pl.ds(at, LANES)
        o_act[:, lanes] = jnp.maximum(
            act[:, lanes].astype(F32) + (rate_active * scale) * total, 0.0).astype(BF16)

    if not direct:
        for c in range(frames // step):
            back(c)
    else:
        half = frames // 2
        quarter = frames // 4
        outer = peers // 2
        inner, far = row % 2, row // 2
        beside = far * 2 + (1 - inner)
        others = [(far + d) % outer for d in range(1, outer)]
        pair = half // outer

        def lanes_at(at, size):
            return pl.ds(pl.multiple_of(at, LANES), size)

        def first_b(to, sender):
            return remote(hs.at[:, lanes_at(half + to * pair, pair)], hb1.at[sender],
                          b1_send.at[to], b1_recv.at[sender], neuron=to * 2 + inner)

        a1 = remote(hs.at[:, lanes_at((1 - inner) * quarter, quarter)], ha1,
                    y_send.at[0], y_recv.at[0], neuron=beside)

        back(1)
        for z in others:
            first_b(z, far).start()
        back(0)
        a1.start()

        def second_a(to, sender):
            return remote(sa.at[:, lanes_at(to * LANES, LANES)], ha2.at[sender],
                          a2_send.at[to], a2_recv.at[sender], neuron=to * 2 + inner)

        b2 = remote(sb.at[:, lanes_at((1 - inner) * LANES, LANES)], hb2,
                    y_send.at[1], y_recv.at[1], neuron=beside)

        def stage_two():
            a1.wait_recv()
            total = ph[:, lanes_at(inner * quarter, quarter)] + whole(ha1[...])
            pa[...] = total
            sa[width:], sa[:width] = centred(total)
            for z in others:
                second_a(z, far).start()
            total = ph[:, lanes_at(half + far * pair, pair)]
            for z in others:
                first_b(far, z).wait_recv()
                total = total + whole(hb1[z])
            pb[...] = total
            sb[width:], sb[:width] = centred(total)
            b2.start()

        def place_a(z, y):
            return pl.multiple_of(y * quarter + z * LANES, LANES)

        def place_b(z, y):
            return pl.multiple_of(half + z * pair + y * LANES, LANES)

        def out_copy(at, send, recv, to):
            piece = o_act.at[:, pl.ds(at, LANES)]
            return remote(piece, piece, send, recv, neuron=to)

        def az(to, owner):
            return out_copy(place_a(owner, inner), oaz_send.at[to], oaz_recv.at[owner],
                            to * 2 + inner)

        def ay(z, y):
            return out_copy(place_a(z, y), oay_send.at[z], oay_recv.at[z], beside)

        def by(y):
            return out_copy(place_b(far, y), y_send.at[2], y_recv.at[2], beside)

        def bz(to, owner, y, slot):
            return out_copy(place_b(owner, y), obz_send.at[slot, to], obz_recv.at[slot, owner],
                            to * 2 + inner)

        def stage_three():
            total = pa[:, lanes_at(far * LANES, LANES)]
            for z in others:
                second_a(far, z).wait_recv()
                total = total + whole(ha2[z])
            fresh(place_a(far, inner), total)
            for z in others:
                az(z, far).start()
            ay(far, inner).start()
            b2.wait_recv()
            fresh(place_b(far, inner), pb[:, lanes_at(inner * LANES, LANES)] + whole(hb2[...]))
            by(inner).start()
            for z in others:
                bz(z, far, inner, 0).start()

        def stage_four():
            by(1 - inner).wait_recv()
            for z in others:
                bz(z, far, 1 - inner, 1).start()
            for z in others:
                az(far, z).wait_recv()
                ay(z, inner).start()

        def stage_five():
            for z in others:
                bz(far, z, inner, 0).wait_recv()
                bz(far, z, 1 - inner, 1).wait_recv()
            for z in range(outer):
                ay(z, 1 - inner).wait_recv()
                ay(z, inner).wait_send()
            for z in others:
                first_b(z, far).wait_send()
                second_a(z, far).wait_send()
                az(z, far).wait_send()
                bz(z, far, inner, 0).wait_send()
                bz(z, far, 1 - inner, 1).wait_send()
            a1.wait_send()
            b2.wait_send()
            by(inner).wait_send()

    def grad(g, buffer):
        base = pl.multiple_of(g * wide, wide)
        buffer[...] = lax.dot_general(
            rext[:, :frames], h_ext[pl.ds(base, wide), :],
            (((1,), (1,)), ((), ())), preferred_element_type=F32)

    grad(diag, gbuf.at[0])
    g_diag = remote(gbuf.at[0], gin.at[0], g_send.at[0], g_recv.at[0], tm=partner)
    g_diag.start()
    if direct:
        stage_two()
    grad(across, gown)
    g_diag.wait_recv()
    total = gown[...] + gin[0]
    mean = jnp.mean(total, axis=1, keepdims=True).astype(BF16)
    gx[:, :wide] = (total - mean.astype(F32)).astype(BF16)
    gx[:, wide:] = jnp.broadcast_to(mean, (rows, LANES))
    g_across = remote(gx, gx_in, g_send.at[1], g_recv.at[1], tm=across)
    g_across.start()
    if direct:
        stage_three()
    grad(partner, gbuf.at[1])
    g_partner = remote(gbuf.at[1], gin.at[1], g_send.at[2], g_recv.at[2], tm=partner)
    g_partner.start()
    if direct:
        stage_four()
    grad(me, gown)
    g_partner.wait_recv()
    g_across.wait_recv()
    back_mean = gx_in[:, wide:].astype(F32)
    for j in range(lags):
        cols = slice(j * width, (j + 1) * width)
        g = gown[:, cols] + gin[1, :, cols] + (gx_in[:, cols].astype(F32) + back_mean)
        g = (rate_motif * scale) * g
        o_mot[j] = jnp.maximum(mot[j].astype(F32) + g[:neurons], 0.0).astype(BF16)
        o_bmot[j] = jnp.maximum(
            bmot[j].astype(F32) + g[neurons:neurons + features], 0.0).astype(BF16)
    if direct:
        stage_five()
    pl.when(me < groups - 1)(act_halo.wait_send)
    pl.when(me > 0)(r_halo.wait_send)
    for copy in (w_across, w_partner, w_relay, g_diag, g_across, g_partner):
        copy.wait_send()


def hand_over(a, b, c, x, y, z, sem):
    copies = [pltpu.make_async_copy(src, dst, sem.at[i])
              for i, (src, dst) in enumerate(((a, x), (b, y), (c, z)))]
    for copy in copies:
        copy.start()
    for copy in copies:
        copy.wait()


def local(peers, groups, data, behaviour, motifs, behav_motifs, activations):
    lags, neurons, width = motifs.shape
    features = behaviour.shape[0]
    frames = activations.shape[1]
    lag_count = lags * groups
    scale = 1.0 / (lag_count * width)
    rate_motif = 0.5 * lag_count * width / math.sqrt(frames * groups)
    rate_active = 0.5 * lag_count * width / math.sqrt(
        lag_count * (neurons * peers + 4 * features * peers))
    rows = neurons + -(-features // 16) * 16
    wide = lags * width
    direct = frames // (2 * peers) == LANES and peers % 2 == 0
    outer = max(peers // 2, 1)
    dma = pltpu.SemaphoreType.DMA
    vmem = pl.BlockSpec(memory_space=pltpu.VMEM)
    flops = 6 * rows * lag_count * width * frames
    scratch = [
        pltpu.VMEM((lag_count * width, frames), BF16),
        pltpu.VMEM((width, frames + LANES), BF16),
        pltpu.VMEM((groups, lags, rows, width), BF16),
        pltpu.VMEM((rows, wide), BF16),
        pltpu.VMEM((groups * width, lags * rows), BF16),
        pltpu.VMEM((rows, frames), F32),
        pltpu.VMEM((rows, frames + LANES), BF16),
        pltpu.VMEM((lags * rows, frames + LANES), BF16),
        pltpu.VMEM((2, rows, wide), F32),
        pltpu.VMEM((2, rows, wide), F32),
        pltpu.VMEM((rows, wide), F32),
        pltpu.VMEM((rows, wide + LANES), BF16),
        pltpu.VMEM((rows, wide + LANES), BF16),
        dma((4,)), dma((3,)), dma((3,)), dma((3,)), dma((3,)),
    ]
    if direct:
        tall, quarter, pair = width + 16, frames // 4, frames // 2 // outer
        scratch += [
            pltpu.VMEM((tall, frames), BF16),
            pltpu.VMEM((width, frames), F32),
            pltpu.VMEM((tall, quarter), BF16),
            pltpu.VMEM((outer, tall, pair), BF16),
            pltpu.VMEM((outer, tall, LANES), BF16),
            pltpu.VMEM((tall, LANES), BF16),
            pltpu.VMEM((tall, quarter), BF16),
            pltpu.VMEM((tall, pair), BF16),
            pltpu.VMEM((width, quarter), F32),
            pltpu.VMEM((width, pair), F32),
            dma((3,)), dma((3,)),
            dma((outer,)), dma((outer,)), dma((outer,)), dma((outer,)),
            dma((outer,)), dma((outer,)), dma((outer,)), dma((outer,)),
            dma((2, outer)), dma((2, outer)),
        ]
    out = pl.pallas_call(
        functools.partial(kernel, peers, direct, scale, rate_motif, rate_active,
                          neurons, features, rows),
        out_shape=(
            jax.ShapeDtypeStruct(motifs.shape, BF16),
            jax.ShapeDtypeStruct(behav_motifs.shape, BF16),
            jax.ShapeDtypeStruct(activations.shape, BF16 if direct else F32),
        ),
        in_specs=[vmem] * 5,
        out_specs=[vmem] * 3,
        scratch_shapes=scratch,
        compiler_params=pltpu.CompilerParams(
            collective_id=0, has_side_effects=True, vmem_limit_bytes=60 * 1024 * 1024),
        cost_estimate=pl.CostEstimate(
            flops=flops, bytes_accessed=4 * 1024 * 1024, transcendentals=0),
    )(data, behaviour, motifs, behav_motifs, activations)
    if direct:
        return pl.pallas_call(
            hand_over,
            out_shape=tuple(jax.ShapeDtypeStruct(o.shape, o.dtype) for o in out),
            in_specs=[pl.BlockSpec(memory_space=pl.ANY)] * 3,
            out_specs=[pl.BlockSpec(memory_space=pl.ANY)] * 3,
            scratch_shapes=[dma((3,))],
        )(*out)
    grad = (rate_active * scale) * lax.psum(out[2], "neuron")
    return out[0], out[1], jnp.maximum(activations.astype(F32) + grad, 0.0).astype(BF16)


def solution(mesh):
    placed = (
        P("neuron", "tm"),
        P("neuron", "tm"),
        P("tm", "neuron", None),
        P("tm", "neuron", None),
        P(None, "tm"),
    )
    return jax.shard_map(
        functools.partial(local, mesh.shape["neuron"], mesh.shape["tm"]),
        mesh=mesh,
        in_specs=placed,
        out_specs=(P("tm", "neuron", None), P("tm", "neuron", None), P(None, "tm")),
        check_vma=False,
    )
```
